32 devices in a mesh: gx: 4 (over z), gy: 2 (over y), gz: 4 (over x, core).
Axes of the slice: x: 2, y: 2, z: 4, core: 2. Of those that a mesh axis runs over, the one named last changes fastest.
Arguments:
- density: float32 [64, 16, 1024], P('gx', 'gy', 'gz'), may hold values from 0.05 to 0.95
- voxel_kind: int32 [64, 16, 1024], P('gx', 'gy', 'gz'), may hold values from 0 to 15, as said below
Outputs:
- new_density: float32 [64, 16, 1024], P('gx', 'gy', 'gz')
- velocity: float32 [64, 16, 1024], P('gx', 'gy', 'gz')
- adjoint: float32 [64, 16, 1024], P('gx', 'gy', 'gz')
The draws below stay inside these ranges and needn't reach their ends.
Inputs may be any that keep to these rules, and one draw needn't show every extreme that they name: `voxel_kind`: 0 to 12 mark design voxels, 13 solid, 14 inlet, 15 outlet.
All inputs are finite; a program needn't handle non-finite values.
Results may differ from the reference program's by a relative error of at most 0.0003.
Values sent between devices are 32-bit elements; how exact they have to be, the bound alone decides.
A program may use at most 128 MiB of HBM per device.

```python
import jax
import jax.numpy as jnp
from jax import lax

RADIUS = 6
LEVELS = 3
CYCLES = 2
COARSE_SWEEPS = 4
BISECT = 9
NX = 64
NY = 16
NZ = 1024


def widen_boxes(values, box_edge):
    values = jnp.repeat(values, box_edge, axis=0)
    values = jnp.repeat(values, box_edge, axis=1)
    return jnp.repeat(values, box_edge, axis=2)


def draw_density(key, part):
    keys = jax.random.split(jax.random.fold_in(key, 11), 1)
    base = jax.random.uniform(keys[0], (NX, NY, NZ), jnp.float32)
    power = jnp.float32(2.5)
    return 0.05 + 0.9 * base ** power


def draw_voxel_kind(key, part):
    box_edge = 8
    box_shape = (NX // box_edge, NY // box_edge, NZ // box_edge)
    keys = jax.random.split(jax.random.fold_in(key, 7), 6)
    level_shift = jax.random.randint(keys[0], (), 0, 4)
    box_solid = jax.random.randint(keys[1], box_shape, 0, 7) + level_shift
    box_inlet = jnp.where(jax.random.randint(keys[2], box_shape, 0, 4) == 0, 3, 0)
    box_outlet = jnp.where(jax.random.randint(keys[3], box_shape, 0, 4) == 0, 3, 0)
    solid_share = widen_boxes(box_solid, box_edge)
    inlet_share = widen_boxes(box_inlet, box_edge)
    outlet_share = widen_boxes(box_outlet, box_edge)
    roll_value = jax.random.randint(keys[4], (NX, NY, NZ), 0, 16)
    design_kind = jax.random.randint(keys[5], (NX, NY, NZ), 0, 13)
    inlet_edge = solid_share + inlet_share
    outlet_edge = inlet_edge + outlet_share
    kind_value = jnp.where(roll_value < solid_share, 13, jnp.where(roll_value < inlet_edge, 14, jnp.where(roll_value < outlet_edge, 15, design_kind)))
    return kind_value.astype(jnp.int32)


def setup_inputs(seed: int = 0) -> dict:
    splits = jax.random.split(jax.random.key(seed), 3)
    density = draw_density(jax.random.fold_in(splits[2], 71), 0)
    voxel_kind = draw_voxel_kind(jax.random.fold_in(splits[2], 71), 0)
    return dict(density=density, voxel_kind=voxel_kind)


penalty_solid = 0.2
penalty_fluid = 0.001
convexity = 0.1
damping = 0.8
step_size = 0.1
move_limit = 0.2
volume_fraction = 0.45
epsilon = 1e-06

def smooth_axis(padded, axis_dim, length):
    result = None
    for offset in range(-RADIUS, RADIUS + 1):
        tap_term = float(RADIUS + 1 - abs(offset)) * lax.slice_in_dim(padded, RADIUS + offset, RADIUS + offset + length, axis=axis_dim)
        result = tap_term if result is None else result + tap_term
    return result

def spread(field_values):
    for axis_dim in range(3):
        widths = [(0, 0), (0, 0), (0, 0)]
        widths[axis_dim] = (RADIUS, RADIUS)
        field_values = smooth_axis(jnp.pad(field_values, widths), axis_dim, field_values.shape[axis_dim])
    return field_values

def edge_sums(cell_count, first_index, grid_total):
    positions = first_index + jnp.arange(cell_count, dtype=jnp.int32)
    result = jnp.zeros((cell_count,), jnp.float32)
    for offset in range(-RADIUS, RADIUS + 1):
        moved = positions + offset
        inside = (moved >= 0) & (moved < grid_total)
        result = result + jnp.where(inside, float(RADIUS + 1 - abs(offset)), 0.0).astype(jnp.float32)
    return result

def operate(field_values, brinkman_penalty, grid_scale):
    padded = jnp.pad(field_values, 1)
    beside = padded[..., 2:, 1:-1, 1:-1] + padded[..., :-2, 1:-1, 1:-1]
    beside = beside + padded[..., 1:-1, 2:, 1:-1] + padded[..., 1:-1, :-2, 1:-1]
    beside = beside + padded[..., 1:-1, 1:-1, 2:] + padded[..., 1:-1, 1:-1, :-2]
    return (6.0 * field_values - beside) * grid_scale + brinkman_penalty * field_values

def relax(field_values, forcing_term, brinkman_penalty, grid_scale, start_blank):
    diagonal = 6.0 * grid_scale + brinkman_penalty
    if start_blank:
        return damping * forcing_term / diagonal
    return field_values + damping * (forcing_term - operate(field_values, brinkman_penalty, grid_scale)) / diagonal

def restrict_grid(field_values):
    shape_a, shape_b, shape_c = field_values.shape[-3:]
    blocks = field_values.reshape(field_values.shape[:-3] + (shape_a // 2, 2, shape_b // 2, 2, shape_c // 2, 2))
    return lax.optimization_barrier(jnp.mean(blocks, axis=(-5, -3, -1)))

def refine(field_values):
    return jnp.repeat(jnp.repeat(jnp.repeat(field_values, 2, axis=-3), 2, axis=-2), 2, axis=-1)

def multilevel_pass(field_values, forcing_term, penalty_pyramid, mesh_depth, start_blank):
    grid_scale = 0.25 ** mesh_depth
    brinkman_penalty = penalty_pyramid[mesh_depth]
    if mesh_depth == LEVELS - 1:
        field_values = relax(None, forcing_term, brinkman_penalty, grid_scale, True)
        for sweep_index in range(COARSE_SWEEPS - 1):
            field_values = relax(field_values, forcing_term, brinkman_penalty, grid_scale, False)
        return field_values
    field_values = relax(field_values, forcing_term, brinkman_penalty, grid_scale, start_blank)
    equation_misfit = forcing_term - operate(field_values, brinkman_penalty, grid_scale)
    coarse_update = multilevel_pass(None, restrict_grid(equation_misfit), penalty_pyramid, mesh_depth + 1, True)
    field_values = field_values + refine(coarse_update)
    return relax(field_values, forcing_term, brinkman_penalty, grid_scale, False)

def compute_velocity(forcing_term, penalty_pyramid):
    field_values = None
    for vcycle_counter in range(CYCLES):
        field_values = multilevel_pass(field_values, forcing_term, penalty_pyramid, 0, vcycle_counter == 0)
    return field_values

def reference(density, voxel_kind):
    design = voxel_kind < 13
    solid_mask = voxel_kind == 13
    inflow_mask = voxel_kind == 14
    outflow_face = voxel_kind == 15
    normal = edge_sums(NX, 0, NX)[:, None, None] * edge_sums(NY, 0, NY)[None, :, None] * edge_sums(NZ, 0, NZ)[None, None, :]
    filtered = spread(density) / normal
    interp = penalty_solid + (penalty_fluid - penalty_solid) * filtered * (1.0 + convexity) / (filtered + convexity)
    brinkman_penalty = jnp.where(design, interp, jnp.where(solid_mask, penalty_solid, penalty_fluid))
    penalty_pyramid = [brinkman_penalty]
    for mesh_depth in range(LEVELS - 1):
        penalty_pyramid.append(restrict_grid(penalty_pyramid[-1]))
    velocity = compute_velocity(inflow_mask.astype(jnp.float32), penalty_pyramid)
    adjoint = compute_velocity(outflow_face.astype(jnp.float32), penalty_pyramid)
    slope = (penalty_fluid - penalty_solid) * (1.0 + convexity) * convexity / ((filtered + convexity) * (filtered + convexity))
    gradient = jnp.where(design, adjoint * velocity * slope, 0.0)
    sensitivity = spread(gradient / normal)
    cell_total = float(NX * NY * NZ)
    scaled = sensitivity / jnp.sqrt(jnp.sum(sensitivity * sensitivity) / cell_total + epsilon)
    target = volume_fraction * jnp.sum(design.astype(jnp.float32))
    trial_base = density - step_size * scaled
    lower_bound = jnp.maximum(0.0, density - move_limit)
    upper_bound = jnp.minimum(1.0, density + move_limit)

    def halve(step_index, bounds):
        low_end, high_end = bounds
        middle = (low_end + high_end) * 0.5
        volume = jnp.sum(jnp.where(design, jnp.clip(trial_base + middle, lower_bound, upper_bound), 0.0))
        above_target = volume > target
        return (jnp.where(above_target, low_end, middle), jnp.where(above_target, middle, high_end))
    low_end, high_end = lax.fori_loop(0, BISECT, halve, (jnp.float32(-2.0), jnp.float32(2.0)))
    multiplier = (low_end + high_end) * 0.5
    new_density = jnp.where(design, jnp.clip(trial_base + multiplier, lower_bound, upper_bound), density)
    return (new_density, velocity, adjoint)
```

```python
import functools

import jax
import jax.numpy as jnp
from jax import lax
from jax.experimental import pallas as pl
from jax.experimental.pallas import tpu as pltpu
from jax.sharding import PartitionSpec as P

RADIUS = 6
LEVELS = 3
CYCLES = 2
COARSE_SWEEPS = 4
BISECT = 9

penalty_solid = 0.2
penalty_fluid = 0.001
convexity = 0.1
damping = 0.8
step_size = 0.1
move_limit = 0.2
volume_fraction = 0.45
epsilon = 1e-06

MESH = pl.DeviceIdType.MESH
F32 = jnp.float32
FIRST = 31
SECOND = 15


def iota(shape, dim):
    return lax.broadcasted_iota(jnp.int32, shape, dim)


def turn(values, shift, dim):
    shift = shift % values.shape[dim]
    return values if shift == 0 else pltpu.roll(values, shift, dim)


def restrict_pair(pair, stride):
    dy, dz = pair.ndim - 2, pair.ndim - 1
    low = ((iota(pair.shape, dy) // stride) & 1) == 0
    pair = pair + jnp.where(low, turn(pair, -stride, dy), turn(pair, stride, dy))
    low = ((iota(pair.shape, dz) // stride) & 1) == 0
    pair = pair + jnp.where(low, turn(pair, -stride, dz), turn(pair, stride, dz))
    return pair * 0.125


def edge_weight(position, total):
    low = jnp.maximum(RADIUS - position, 0)
    high = jnp.maximum(RADIUS - (total - 1 - position), 0)
    top = (RADIUS + 1) ** 2
    return (top - ((low * (low + 1)) >> 1) - ((high * (high + 1)) >> 1)).astype(F32)


def box(values, count):
    two = values[:-1] + values[1:]
    four = two[:-2] + two[2:]
    return four[:count] + two[4 : 4 + count] + values[6 : 6 + count]


def kernel(
    counts, density, kind, new_density, velocity, adjoint,
    field, filtered, normal, weight_y, weight_z,
    fx_lo, fx_hi, fy_lo, fy_hi, fz_out, fz_lo, fz_hi, f_send, f_recv,
    v0a, v0b, s0, diag0, damp0, v1a, v1b, s1, diag1, damp1, v2a, v2b, s2, damp2,
    mx_lo, mx_hi, my_out, my_lo, my_hi, mz_out, mz_lo, mz_hi, m_send, m_recv,
    q_part, q_one, q_mid, q_two, a_part, a_one, a_mid, a_two, b_part, b_one, b_mid, b_two,
    r_send, r_recv,
):
    nx, ny, nz = density.shape
    cx, cy, cz = counts
    ix, iy, iz = lax.axis_index("gx"), lax.axis_index("gy"), lax.axis_index("gz")
    group = cy * cz
    place = iy * cz + iz

    def group_peer(step):
        other = lax.rem(place + step, group)
        return {"gy": other // cz, "gz": lax.rem(other, cz)}

    def line_peer(step):
        return {"gx": lax.rem(ix + step, cx)}

    has_up = (ix < cx - 1, iy < cy - 1, iz < cz - 1)
    has_down = (ix > 0, iy > 0, iz > 0)
    names = ("gx", "gy", "gz")
    index = (ix, iy, iz)

    def clear(absent, refs):
        @pl.when(jnp.logical_not(absent))
        def _():
            for ref in refs:
                ref[...] = jnp.zeros(ref.shape, F32)

    clear(has_down[0], (fx_lo, mx_lo))
    clear(has_up[0], (fx_hi, mx_hi))
    clear(has_down[1], (fy_lo, my_lo))
    clear(has_up[1], (fy_hi, my_hi))
    clear(has_down[2], (fz_lo, mz_lo))
    clear(has_up[2], (fz_hi, mz_hi))

    barrier = pltpu.get_barrier_semaphore()
    for step in range(1, group):
        pl.semaphore_signal(barrier, inc=1, device_id=group_peer(step), device_id_type=MESH)
    for step in range(1, cx):
        pl.semaphore_signal(barrier, inc=1, device_id=line_peer(step), device_id_type=MESH)

    field[...] = density[...]
    shape = (nx, ny, nz)
    normal[...] = 1.0 / (
        edge_weight(iota(shape, 0) + ix * nx, cx * nx)
        * edge_weight(iota(shape, 1) + iy * ny, cy * ny)
        * edge_weight(iota(shape, 2) + iz * nz, cz * nz)
    )
    rows = nx * ny
    r, c = iota((rows, 3 * rows), 0), iota((rows, 3 * rows), 1)
    block = c // rows
    inner = c - block * rows
    gap = jnp.abs((block - 1) * ny + inner % ny - r % ny)
    weight_y[...] = jnp.where(
        inner // ny == r // ny, jnp.maximum(RADIUS + 1 - gap, 0), 0
    ).astype(F32)
    r, c = iota((nz + 128, nz), 0), iota((nz + 128, nz), 1)
    at = jnp.where(r < 8, nz + r, jnp.where(r < 120, -1000, r - 128))
    weight_z[...] = jnp.maximum(RADIUS + 1 - jnp.abs(at - c), 0).astype(F32)
    for plane in range(nx):
        s0[plane] = jnp.stack(
            [(kind[plane] == 14).astype(F32), (kind[plane] == 15).astype(F32)]
        )

    pl.semaphore_wait(barrier, group - 1 + cx - 1)

    def swap(sends, send_sems, recv_sems):
        copies = []
        for axis, up_src, up_dst, down_src, down_dst in sends:
            for way, src, dst in ((0, up_src, up_dst), (1, down_src, down_dst)):
                def make(axis=axis, way=way, src=src, dst=dst):
                    to = index[axis] + 1 - 2 * way
                    return pltpu.make_async_remote_copy(
                        src_ref=src,
                        dst_ref=dst,
                        send_sem=send_sems.at[2 * axis + way],
                        recv_sem=recv_sems.at[2 * axis + way],
                        device_id={names[axis]: to},
                        device_id_type=MESH,
                    )
                sent = (has_up, has_down)[way][axis]
                got = (has_down, has_up)[way][axis]
                copies.append((make, sent, got))

        for make, sent, got in copies:
            @pl.when(sent)
            def _(make=make):
                make().start()

        for make, sent, got in copies:
            @pl.when(got)
            def _(make=make):
                make().wait_recv()

        for make, sent, got in copies:
            @pl.when(sent)
            def _(make=make):
                make().wait_send()

    def pack_z(source, planes, out):
        tail = head = None
        for plane in range(planes):
            full = source[plane]
            dim = full.ndim - 1
            last = turn(full[..., nz - 128 :], 8 * plane + 8, dim)
            first = turn(full[..., :128], 8 * plane, dim)
            mine = (iota(last.shape, dim) >> 3) == plane
            tail = last if tail is None else jnp.where(mine, last, tail)
            head = first if head is None else jnp.where(mine, first, head)
        out[0] = tail
        out[1] = head

    def spread():
        swap(
            [(0, field.at[pl.ds(nx - RADIUS, RADIUS)], fx_lo, field.at[pl.ds(0, RADIUS)], fx_hi)],
            f_send, f_recv,
        )
        padded = jnp.concatenate([fx_lo[...], field[...], fx_hi[...]], axis=0)
        field[...] = box(box(padded, nx + RADIUS), nx)
        swap([(1, field, fy_lo, field, fy_hi)], f_send, f_recv)
        padded = jnp.concatenate(
            [ref[...].reshape(rows, nz) for ref in (fy_lo, field, fy_hi)], axis=0
        )
        field[...] = jnp.dot(
            weight_y[...], padded, precision=lax.Precision.HIGHEST, preferred_element_type=F32
        ).reshape(nx, ny, nz)
        pack_z(field, nx, fz_out)
        swap([(2, fz_out.at[0], fz_lo, fz_out.at[1], fz_hi)], f_send, f_recv)
        lane = iota((ny, 128), 1)
        parts = []
        for plane in range(nx):
            low = turn(fz_lo[...], 120 - 8 * plane, 1)
            high = turn(fz_hi[...], -8 * plane, 1)
            beside = jnp.where(lane >= 120, low, jnp.where(lane < 8, high, 0.0))
            parts.append(jnp.concatenate([beside, field[plane]], axis=1))
        padded = jnp.concatenate(parts, axis=0)
        field[...] = jnp.dot(
            padded, weight_z[...], precision=lax.Precision.HIGHEST, preferred_element_type=F32
        ).reshape(nx, ny, nz)

    spread()
    smooth = field[...] * normal[...]
    filtered[...] = smooth
    interp = penalty_solid + (penalty_fluid - penalty_solid) * smooth * (1.0 + convexity) / (
        smooth + convexity
    )
    kinds = kind[...]
    penalty = jnp.where(
        kinds < 13, interp, jnp.where(kinds == 13, penalty_solid, penalty_fluid)
    )
    diag0[...] = 6.0 + penalty
    damp0[...] = damping / (6.0 + penalty)
    level1 = []
    for plane in range(nx // 2):
        coarse = restrict_pair(penalty[2 * plane] + penalty[2 * plane + 1], 1)
        level1.append(coarse)
        diag1[plane] = 1.5 + coarse
        damp1[plane] = damping / (1.5 + coarse)
    for plane in range(nx // 4):
        coarse = restrict_pair(level1[2 * plane] + level1[2 * plane + 1], 2)
        damp2[plane] = damping / (0.375 + coarse)

    sub = iota((2, ny, nz), 1)
    lane = iota((2, ny, 128), 2)
    rounds = [0]

    def exchange(source, planes):
        parity = rounds[0] % 2
        rounds[0] += 1
        for plane in range(planes):
            for which in range(2):
                row = 2 * plane + which
                my_out[parity, 0, row : row + 1] = source[plane, which, ny - 1 : ny]
                my_out[parity, 1, row : row + 1] = source[plane, which, 0:1]
        pack_z(source, planes, mz_out.at[parity])
        part = pl.ds(0, 2 * planes)
        swap(
            [
                (0, source.at[planes - 1], mx_lo.at[parity], source.at[0], mx_hi.at[parity]),
                (1, my_out.at[parity, 0, part], my_lo.at[parity, part],
                 my_out.at[parity, 1, part], my_hi.at[parity, part]),
                (2, mz_out.at[parity, 0], mz_lo.at[parity],
                 mz_out.at[parity, 1], mz_hi.at[parity]),
            ],
            m_send.at[parity], m_recv.at[parity],
        )
        return parity

    def both(ref, parity, plane):
        return jnp.stack(
            [
                jnp.broadcast_to(ref[parity, 2 * plane + which : 2 * plane + which + 1], (ny, nz))
                for which in range(2)
            ]
        )

    def beside(source, planes, stride, parity, plane):
        centre = source[plane]
        low = source[plane - 1] if plane else mx_lo[parity]
        high = source[plane + 1] if plane < planes - 1 else mx_hi[parity]
        total = low + high
        low = jnp.where(sub < stride, both(my_lo, parity, plane), turn(centre, stride, 1))
        high = jnp.where(sub >= ny - stride, both(my_hi, parity, plane), turn(centre, -stride, 1))
        total = total + low + high
        low = turn(centre, stride, 2)
        edge = turn(mz_lo[parity], stride - 8 - 8 * plane, 2)
        low = jnp.concatenate(
            [jnp.where(lane < stride, edge, low[..., :128]), low[..., 128:]], axis=2
        )
        high = turn(centre, -stride, 2)
        edge = turn(mz_hi[parity], 128 - stride - 8 * plane, 2)
        high = jnp.concatenate(
            [high[..., : nz - 128], jnp.where(lane >= 128 - stride, edge, high[..., nz - 128 :])],
            axis=2,
        )
        return total + low + high

    def relax(source, target, forcing, damp, planes, stride, scale):
        parity = exchange(source, planes)
        for plane in range(planes):
            total = beside(source, planes, stride, parity, plane)
            target[plane] = (1.0 - damping) * source[plane] + damp[plane][None] * (
                forcing[plane] + scale * total
            )

    def misfit(source, coarse, forcing, diag, planes, stride, scale):
        parity = exchange(source, planes)
        for pair in range(planes // 2):
            total = None
            for plane in (2 * pair, 2 * pair + 1):
                rest = (
                    forcing[plane]
                    - diag[plane][None] * source[plane]
                    + scale * beside(source, planes, stride, parity, plane)
                )
                total = rest if total is None else total + rest
            coarse[pair] = restrict_pair(total, stride)

    now, later = v0a, v0b
    for cycle in range(CYCLES):
        if cycle == 0:
            for plane in range(nx):
                now[plane] = damp0[plane][None] * s0[plane]
        else:
            relax(now, later, s0, damp0, nx, 1, 1.0)
            now, later = later, now
        misfit(now, s1, s0, diag0, nx, 1, 1.0)
        for plane in range(nx // 2):
            v1a[plane] = damp1[plane][None] * s1[plane]
        misfit(v1a, s2, s1, diag1, nx // 2, 2, 0.25)
        for plane in range(nx // 4):
            v2a[plane] = damp2[plane][None] * s2[plane]
        here, there = v2a, v2b
        for sweep in range(COARSE_SWEEPS - 1):
            relax(here, there, s2, damp2, nx // 4, 4, 0.0625)
            here, there = there, here
        for plane in range(nx // 2):
            v1a[plane] = v1a[plane] + here[plane // 2]
        relax(v1a, v1b, s1, damp1, nx // 2, 2, 0.25)
        for plane in range(nx):
            now[plane] = now[plane] + v1b[plane // 2]
        relax(now, later, s0, damp0, nx, 1, 1.0)
        now, later = later, now

    for plane in range(nx):
        flow, dual = now[plane, 0], now[plane, 1]
        velocity[plane] = flow
        adjoint[plane] = dual
        bent = filtered[plane] + convexity
        slope = (penalty_fluid - penalty_solid) * (1.0 + convexity) * convexity / (bent * bent)
        field[plane] = jnp.where(kind[plane] < 13, dual * flow * slope, 0.0) * normal[plane]
    spread()

    sems = [0]

    def total_of(part, one, mid, two):
        def stage(source, target, size, mine, peer):
            copies = []
            for step in range(1, size):
                copy = pltpu.make_async_remote_copy(
                    src_ref=source,
                    dst_ref=target.at[mine],
                    send_sem=r_send.at[sems[0]],
                    recv_sem=r_recv.at[sems[0]],
                    device_id=peer(step),
                    device_id_type=MESH,
                )
                sems[0] += 1
                copy.start()
                copies.append(copy)
            target[mine] = source[...]
            for copy in copies:
                copy.wait_recv()
            total = target[0]
            for other in range(1, size):
                total = total + target[other]
            for copy in copies:
                copy.wait_send()
            return total

        mid[...] = stage(part, one, group, place, group_peer)
        return stage(mid, two, cx, ix, line_peer)

    def fold(values):
        values = jnp.sum(values, axis=0)
        total = values[:, :128]
        for start in range(128, nz, 128):
            total = total + values[:, start : start + 128]
        return total

    def whole(values):
        return jnp.sum(jnp.sum(values, axis=0, keepdims=True), axis=1, keepdims=True)

    design = kind[...] < 13
    sensitivity = field[...]
    q_part[0:8] = fold(sensitivity * sensitivity)
    q_part[8:16] = fold(design.astype(F32))
    stats = total_of(q_part, q_one, q_mid, q_two)
    cells = float(cx * nx * cy * ny * cz * nz)
    spreading = jnp.sqrt(whole(stats[0:8]) / cells + epsilon)
    target = volume_fraction * whole(stats[8:16])
    old = density[...]
    field[...] = old - step_size * (field[...] / spreading[None])
    base = jnp.where(design, field[...], 0.0)
    lower = jnp.where(design, jnp.maximum(0.0, old - move_limit), 0.0)
    upper = jnp.where(design, jnp.minimum(1.0, old + move_limit), 0.0)
    v0a[:, 0] = base
    v0a[:, 1] = lower
    v0b[:, 0] = upper

    def narrow(start, width, trials, part, one, mid, two):
        step = width / (trials + 1)
        part[...] = jnp.zeros(part.shape, F32)
        for trial in range(trials):
            middle = start + (trial + 1) * step
            tried = jnp.minimum(jnp.maximum(v0a[:, 0] + middle[None], v0a[:, 1]), v0b[:, 0])
            part[trial : trial + 1] = jnp.sum(fold(tried), axis=0, keepdims=True)
        volumes = jnp.sum(total_of(part, one, mid, two), axis=1, keepdims=True)
        kept = (iota(volumes.shape, 0) < trials) & jnp.logical_not(volumes > target)
        below = jnp.sum(kept.astype(F32), axis=0, keepdims=True)
        return start + below * step, step

    start, width = jnp.full((1, 1), -2.0, F32), 4.0
    start, width = narrow(start, width, FIRST, a_part, a_one, a_mid, a_two)
    start, width = narrow(start, width, SECOND, b_part, b_one, b_mid, b_two)
    multiplier = start + width * 0.5
    lower = jnp.maximum(0.0, old - move_limit)
    upper = jnp.minimum(1.0, old + move_limit)
    new_density[...] = jnp.where(
        design, jnp.minimum(jnp.maximum(field[...] + multiplier[None], lower), upper), old
    )


def body(counts, density, kind):
    nx, ny, nz = density.shape
    cx, cy, cz = counts
    group = cy * cz
    sends = 3 * (group - 1 + cx - 1)
    vm = lambda *shape: pltpu.VMEM(shape, F32)
    dma = lambda *shape: pltpu.SemaphoreType.DMA(shape)
    cube = (nx, ny, nz)
    half = (nx // 2, ny, nz)
    quarter = (nx // 4, ny, nz)
    pair = lambda planes: vm(planes, 2, ny, nz)

    def sums(count):
        return [vm(count, 128), vm(group, count, 128), vm(count, 128), vm(cx, count, 128)]

    scratch = [
        vm(*cube), vm(*cube), vm(*cube), vm(nx * ny, 3 * nx * ny), vm(nz + 128, nz),
        vm(RADIUS, ny, nz), vm(RADIUS, ny, nz), vm(*cube), vm(*cube),
        vm(2, ny, 128), vm(ny, 128), vm(ny, 128), dma(6), dma(6),
        pair(nx), pair(nx), pair(nx), vm(*cube), vm(*cube),
        pair(nx // 2), pair(nx // 2), pair(nx // 2), vm(*half), vm(*half),
        pair(nx // 4), pair(nx // 4), pair(nx // 4), vm(*quarter),
        vm(2, 2, ny, nz), vm(2, 2, ny, nz),
        vm(2, 2, 2 * nx, nz), vm(2, 2 * nx, nz), vm(2, 2 * nx, nz),
        vm(2, 2, 2, ny, 128), vm(2, 2, ny, 128), vm(2, 2, ny, 128), dma(2, 6), dma(2, 6),
        *sums(16), *sums(FIRST + 1), *sums(SECOND + 1),
        dma(sends), dma(sends),
    ]
    spec = pl.BlockSpec(memory_space=pltpu.VMEM)
    return pl.pallas_call(
        functools.partial(kernel, counts),
        out_shape=[jax.ShapeDtypeStruct(cube, F32)] * 3,
        in_specs=[spec] * 2,
        out_specs=[spec] * 3,
        scratch_shapes=scratch,
        compiler_params=pltpu.CompilerParams(
            collective_id=0, has_side_effects=True, vmem_limit_bytes=40 * 1024 * 1024
        ),
    )(density, kind)


def solution(mesh):
    counts = tuple(mesh.shape[name] for name in ("gx", "gy", "gz"))

    def run(density, kind):
        return tuple(body(counts, density, kind))

    return jax.shard_map(
        run,
        mesh=mesh,
        in_specs=(P("gx", "gy", "gz"), P("gx", "gy", "gz")),
        out_specs=(P("gx", "gy", "gz"), P("gx", "gy", "gz"), P("gx", "gy", "gz")),
        check_vma=False,
    )
```

```python
import functools

import jax
import jax.numpy as jnp
from jax import lax
from jax.experimental import pallas as pl
from jax.experimental.pallas import tpu as pltpu
from jax.sharding import PartitionSpec as P

RADIUS = 6
LEVELS = 3
CYCLES = 2
COARSE_SWEEPS = 4
BISECT = 9

penalty_solid = 0.2
penalty_fluid = 0.001
convexity = 0.1
damping = 0.8
step_size = 0.1
move_limit = 0.2
volume_fraction = 0.45
epsilon = 1e-06

MESH = pl.DeviceIdType.MESH
F32 = jnp.float32
FIRST = 31
SECOND = 15


def iota(shape, dim):
    return lax.broadcasted_iota(jnp.int32, shape, dim)


def turn(values, shift, dim):
    shift = shift % values.shape[dim]
    return values if shift == 0 else pltpu.roll(values, shift, dim)


def restrict_pair(pair, stride):
    dy, dz = pair.ndim - 2, pair.ndim - 1
    low = ((iota(pair.shape, dy) // stride) & 1) == 0
    pair = pair + jnp.where(low, turn(pair, -stride, dy), turn(pair, stride, dy))
    low = ((iota(pair.shape, dz) // stride) & 1) == 0
    pair = pair + jnp.where(low, turn(pair, -stride, dz), turn(pair, stride, dz))
    return pair * 0.125


def edge_weight(position, total):
    low = jnp.maximum(RADIUS - position, 0)
    high = jnp.maximum(RADIUS - (total - 1 - position), 0)
    top = (RADIUS + 1) ** 2
    return (top - ((low * (low + 1)) >> 1) - ((high * (high + 1)) >> 1)).astype(F32)


def kernel(
    counts, density, kind, new_density, velocity, adjoint,
    field, filtered, normal, weight_y, weight_z,
    padded, fz_out, fz_in, f_send, f_recv,
    v0a, v0b, s0, diag0, damp0, v1a, v1b, s1, diag1, damp1, v2a, v2b, s2, damp2,
    mx_lo, mx_hi, my_out, my_lo, my_hi, mz_out, mz_lo, mz_hi, m_send, m_recv,
    a_part, b_part, r_out, r_mid, r_one, r_two, r_send, r_recv,
):
    nx, ny, nz = density.shape
    cx, cy, cz = counts
    ix, iy, iz = lax.axis_index("gx"), lax.axis_index("gy"), lax.axis_index("gz")
    lines, one_stage = plan_sums(counts)
    if one_stage:
        places = ((ix * cy + iy) * cz + iz,)
    else:
        places = (iy * cz + iz, ix)
    plane_size = cy * cz

    def device_of(flat):
        rest = lax.rem(flat, plane_size)
        return {"gx": flat // plane_size, "gy": rest // cz, "gz": lax.rem(rest, cz)}

    def peer_of(stage, step):
        if one_stage:
            return device_of(lax.rem(places[0] + step, lines[0]))
        if stage == 0:
            other = lax.rem(places[0] + step, lines[0])
            return {"gy": other // cz, "gz": lax.rem(other, cz)}
        return {"gx": lax.rem(ix + step, cx)}

    has_up = (ix < cx - 1, iy < cy - 1, iz < cz - 1)
    has_down = (ix > 0, iy > 0, iz > 0)
    names = ("gx", "gy", "gz")
    index = (ix, iy, iz)

    def clear(absent, refs):
        @pl.when(jnp.logical_not(absent))
        def _():
            for ref in refs:
                ref[...] = jnp.zeros(ref.shape, F32)

    clear(has_down[0], (mx_lo,))
    clear(has_up[0], (mx_hi,))
    clear(has_down[1], (my_lo,))
    clear(has_up[1], (my_hi,))
    clear(has_down[2], (mz_lo,))
    clear(has_up[2], (mz_hi,))
    padded[...] = jnp.zeros(padded.shape, F32)
    fz_in[...] = jnp.zeros(fz_in.shape, F32)

    barrier = pltpu.get_barrier_semaphore()
    devices = cx * cy * cz
    me = (ix * cy + iy) * cz + iz

    def greet(step):
        other = device_of(lax.rem(me + step, devices))
        pl.semaphore_signal(barrier, inc=1, device_id=other, device_id_type=MESH)

    if one_stage:
        for step in range(1, devices):
            greet(step)
    else:
        lax.fori_loop(1, devices, lambda step, none: (greet(step), none)[1], 0)

    field[...] = density[...]
    shape = (nx, ny, nz)
    normal[...] = 1.0 / (
        edge_weight(iota(shape, 0) + ix * nx, cx * nx)
        * edge_weight(iota(shape, 1) + iy * ny, cy * ny)
        * edge_weight(iota(shape, 2) + iz * nz, cz * nz)
    )
    rows = nx * ny
    wide = nx + 2 * RADIUS
    r, c = iota((rows, 3 * wide * ny), 0), iota((rows, 3 * wide * ny), 1)
    block = c // (wide * ny)
    inner = c - block * (wide * ny)
    gap_y = jnp.abs((block - 1) * ny + inner % ny - r % ny)
    gap_x = jnp.abs(inner // ny - RADIUS - r // ny)
    top = RADIUS + 1
    weight_y[...] = (jnp.maximum(top - gap_y, 0) * jnp.maximum(top - gap_x, 0)).astype(F32)
    r, c = iota((nz + 128, nz), 0), iota((nz + 128, nz), 1)
    at = jnp.where(r < 8, nz + r, jnp.where(r < 120, -1000, r - 128))
    weight_z[...] = jnp.maximum(RADIUS + 1 - jnp.abs(at - c), 0).astype(F32)
    for plane in range(nx):
        s0[plane] = jnp.stack(
            [(kind[plane] == 14).astype(F32), (kind[plane] == 15).astype(F32)]
        )

    pl.semaphore_wait(barrier, devices - 1)

    def swap(sends, send_sems, recv_sems):
        copies = []
        for axis, up_src, up_dst, down_src, down_dst in sends:
            for way, src, dst in ((0, up_src, up_dst), (1, down_src, down_dst)):
                def make(axis=axis, way=way, src=src, dst=dst):
                    to = index[axis] + 1 - 2 * way
                    return pltpu.make_async_remote_copy(
                        src_ref=src,
                        dst_ref=dst,
                        send_sem=send_sems.at[2 * axis + way],
                        recv_sem=recv_sems.at[2 * axis + way],
                        device_id={names[axis]: to},
                        device_id_type=MESH,
                    )
                sent = (has_up, has_down)[way][axis]
                got = (has_down, has_up)[way][axis]
                copies.append((make, sent, got))

        for make, sent, got in copies:
            @pl.when(sent)
            def _(make=make):
                make().start()

        for make, sent, got in copies:
            @pl.when(got)
            def _(make=make):
                make().wait_recv()

        for make, sent, got in copies:
            @pl.when(sent)
            def _(make=make):
                make().wait_send()

    def pack_z(source, planes, out):
        tail = head = None
        for plane in range(planes):
            full = source[plane]
            dim = full.ndim - 1
            last = turn(full[..., nz - 128 :], 8 * plane + 8, dim)
            first = turn(full[..., :128], 8 * plane, dim)
            mine = (iota(last.shape, dim) >> 3) == plane
            tail = last if tail is None else jnp.where(mine, last, tail)
            head = first if head is None else jnp.where(mine, first, head)
        out[0] = tail
        out[1] = head

    ways = [
        (dx, dy, dz)
        for dz in (0, 1, -1) for dx in (0, 1, -1) for dy in (1, -1, 0) if (dx, dy, dz) != (0, 0, 0)
    ]

    def reachable(way, sign):
        there = None
        for axis in range(3):
            if way[axis]:
                side = (has_up if way[axis] * sign > 0 else has_down)[axis]
                there = side if there is None else jnp.logical_and(there, side)
        return there

    def spread():
        padded[1, RADIUS : RADIUS + nx, :, 128:] = field[...]
        pack_z(field, nx, fz_out)

        def make(number, way):
            dx, dy, dz = way
            if dz == 0:
                start = nx - RADIUS if dx > 0 else 0
                at = 0 if dx > 0 else RADIUS + nx if dx < 0 else RADIUS
                size = RADIUS if dx else nx
                src = field.at[pl.ds(start, size)]
                dst = padded.at[1 - dy, pl.ds(at, size), :, pl.ds(128, nz)]
            else:
                which = 0 if dz > 0 else 1
                src = fz_out.at[which]
                dst = fz_in.at[which, 1 - dy, 1 - dx]
            there = {names[axis]: index[axis] + way[axis] for axis in range(3) if way[axis]}
            return pltpu.make_async_remote_copy(
                src_ref=src, dst_ref=dst, send_sem=f_send.at[number],
                recv_sem=f_recv.at[number], device_id=there, device_id_type=MESH,
            )

        for number, way in enumerate(ways):
            @pl.when(reachable(way, 1))
            def _(number=number, way=way):
                make(number, way).start()

        for number, way in reversed(list(enumerate(ways))):
            @pl.when(reachable(way, -1))
            def _(number=number, way=way):
                make(number, way).wait_recv()

        for number, way in enumerate(ways):
            @pl.when(reachable(way, 1))
            def _(number=number, way=way):
                make(number, way).wait_send()

        lane = iota((ny, 128), 1)
        for dy in range(3):
            for plane in range(wide):
                if plane < RADIUS:
                    dx, origin = 0, nx - RADIUS + plane
                elif plane < RADIUS + nx:
                    dx, origin = 1, plane - RADIUS
                else:
                    dx, origin = 2, plane - RADIUS - nx
                low = turn(fz_in[0, dy, dx], 120 - 8 * origin, 1)
                high = turn(fz_in[1, dy, dx], -8 * origin, 1)
                padded[dy, plane, :, 0:128] = jnp.where(
                    lane >= 120, low, jnp.where(lane < 8, high, 0.0)
                )
        mixed = jnp.dot(
            weight_y[...], padded[...].reshape(3 * wide * ny, nz + 128),
            precision=lax.Precision.HIGHEST, preferred_element_type=F32,
        )
        field[...] = jnp.dot(
            mixed, weight_z[...], precision=lax.Precision.HIGHEST, preferred_element_type=F32
        ).reshape(nx, ny, nz)

    spread()
    smooth = field[...] * normal[...]
    filtered[...] = smooth
    interp = penalty_solid + (penalty_fluid - penalty_solid) * smooth * (1.0 + convexity) / (
        smooth + convexity
    )
    kinds = kind[...]
    penalty = jnp.where(
        kinds < 13, interp, jnp.where(kinds == 13, penalty_solid, penalty_fluid)
    )
    diag0[...] = 6.0 + penalty
    damp0[...] = damping / (6.0 + penalty)
    level1 = []
    for plane in range(nx // 2):
        coarse = restrict_pair(penalty[2 * plane] + penalty[2 * plane + 1], 1)
        level1.append(coarse)
        diag1[plane] = 1.5 + coarse
        damp1[plane] = damping / (1.5 + coarse)
    for plane in range(nx // 4):
        coarse = restrict_pair(level1[2 * plane] + level1[2 * plane + 1], 2)
        damp2[plane] = damping / (0.375 + coarse)

    sub = iota((2, ny, nz), 1)
    lane = iota((2, ny, 128), 2)
    rounds = [0]

    def exchange(source, planes):
        parity = rounds[0] % 2
        rounds[0] += 1
        for plane in range(planes):
            for which in range(2):
                row = 2 * plane + which
                my_out[parity, 0, row : row + 1] = source[plane, which, ny - 1 : ny]
                my_out[parity, 1, row : row + 1] = source[plane, which, 0:1]
        pack_z(source, planes, mz_out.at[parity])
        part = pl.ds(0, 2 * planes)
        swap(
            [
                (0, source.at[planes - 1], mx_lo.at[parity], source.at[0], mx_hi.at[parity]),
                (1, my_out.at[parity, 0, part], my_lo.at[parity, part],
                 my_out.at[parity, 1, part], my_hi.at[parity, part]),
                (2, mz_out.at[parity, 0], mz_lo.at[parity],
                 mz_out.at[parity, 1], mz_hi.at[parity]),
            ],
            m_send.at[parity], m_recv.at[parity],
        )
        return parity

    def both(ref, parity, plane):
        return jnp.stack(
            [
                jnp.broadcast_to(ref[parity, 2 * plane + which : 2 * plane + which + 1], (ny, nz))
                for which in range(2)
            ]
        )

    def beside(source, planes, stride, parity, plane):
        centre = source[plane]
        low = source[plane - 1] if plane else mx_lo[parity]
        high = source[plane + 1] if plane < planes - 1 else mx_hi[parity]
        total = low + high
        low = jnp.where(sub < stride, both(my_lo, parity, plane), turn(centre, stride, 1))
        high = jnp.where(sub >= ny - stride, both(my_hi, parity, plane), turn(centre, -stride, 1))
        total = total + low + high
        low = turn(centre, stride, 2)
        edge = turn(mz_lo[parity], stride - 8 - 8 * plane, 2)
        low = jnp.concatenate(
            [jnp.where(lane < stride, edge, low[..., :128]), low[..., 128:]], axis=2
        )
        high = turn(centre, -stride, 2)
        edge = turn(mz_hi[parity], 128 - stride - 8 * plane, 2)
        high = jnp.concatenate(
            [high[..., : nz - 128], jnp.where(lane >= 128 - stride, edge, high[..., nz - 128 :])],
            axis=2,
        )
        return total + low + high

    def relax(source, target, forcing, damp, planes, stride, scale):
        parity = exchange(source, planes)
        for plane in range(planes):
            total = beside(source, planes, stride, parity, plane)
            target[plane] = (1.0 - damping) * source[plane] + damp[plane][None] * (
                forcing[plane] + scale * total
            )

    def misfit(source, coarse, forcing, diag, planes, stride, scale):
        parity = exchange(source, planes)
        for pair in range(planes // 2):
            total = None
            for plane in (2 * pair, 2 * pair + 1):
                rest = (
                    forcing[plane]
                    - diag[plane][None] * source[plane]
                    + scale * beside(source, planes, stride, parity, plane)
                )
                total = rest if total is None else total + rest
            coarse[pair] = restrict_pair(total, stride)

    now, later = v0a, v0b
    for cycle in range(CYCLES):
        if cycle == 0:
            for plane in range(nx):
                now[plane] = damp0[plane][None] * s0[plane]
        else:
            relax(now, later, s0, damp0, nx, 1, 1.0)
            now, later = later, now
        misfit(now, s1, s0, diag0, nx, 1, 1.0)
        for plane in range(nx // 2):
            v1a[plane] = damp1[plane][None] * s1[plane]
        misfit(v1a, s2, s1, diag1, nx // 2, 2, 0.25)
        for plane in range(nx // 4):
            v2a[plane] = damp2[plane][None] * s2[plane]
        here, there = v2a, v2b
        for sweep in range(COARSE_SWEEPS - 1):
            relax(here, there, s2, damp2, nx // 4, 4, 0.0625)
            here, there = there, here
        for plane in range(nx // 2):
            v1a[plane] = v1a[plane] + here[plane // 2]
        relax(v1a, v1b, s1, damp1, nx // 2, 2, 0.25)
        for plane in range(nx):
            now[plane] = now[plane] + v1b[plane // 2]
        relax(now, later, s0, damp0, nx, 1, 1.0)
        now, later = later, now

    for plane in range(nx):
        flow, dual = now[plane, 0], now[plane, 1]
        velocity[plane] = flow
        adjoint[plane] = dual
        bent = filtered[plane] + convexity
        slope = (penalty_fluid - penalty_solid) * (1.0 + convexity) * convexity / (bent * bent)
        field[plane] = jnp.where(kind[plane] < 13, dual * flow * slope, 0.0) * normal[plane]
    spread()

    sems = [0]

    def total_of(number, row):
        for stage, size in enumerate(lines):
            source = (r_out, r_mid)[stage].at[number]
            target = (r_one, r_two)[stage].at[number]
            source[...] = row
            copies = []
            for step in range(1, size):
                copy = pltpu.make_async_remote_copy(
                    src_ref=source,
                    dst_ref=target.at[places[stage]],
                    send_sem=r_send.at[sems[0]],
                    recv_sem=r_recv.at[sems[0]],
                    device_id=peer_of(stage, step),
                    device_id_type=MESH,
                )
                sems[0] += 1
                copy.start()
                copies.append(copy)
            target[places[stage]] = row
            for copy in copies:
                copy.wait_recv()
            row = target[0]
            for other in range(1, size):
                row = row + target[other]
            for copy in copies:
                copy.wait_send()
        return row

    def fold(values):
        values = jnp.sum(values, axis=0)
        total = values[:, :128]
        for start in range(128, nz, 128):
            total = total + values[:, start : start + 128]
        return total

    def whole(values):
        return jnp.sum(jnp.sum(values, axis=0, keepdims=True), axis=1, keepdims=True)

    design = kind[...] < 13
    sensitivity = field[...]
    spot = iota((1, 128), 1)
    squares = whole(fold(sensitivity * sensitivity))
    designs = whole(fold(design.astype(F32)))
    stats = total_of(0, jnp.where(spot == 0, squares, jnp.where(spot == 1, designs, 0.0)))
    cells = float(cx * nx * cy * ny * cz * nz)
    spreading = jnp.sqrt(whole(jnp.where(spot == 0, stats, 0.0)) / cells + epsilon)
    target = volume_fraction * whole(jnp.where(spot == 1, stats, 0.0))
    old = density[...]
    field[...] = old - step_size * (field[...] / spreading[None])
    base = jnp.where(design, field[...], 0.0)
    lower = jnp.where(design, jnp.maximum(0.0, old - move_limit), 0.0)
    upper = jnp.where(design, jnp.minimum(1.0, old + move_limit), 0.0)
    v0a[:, 0] = base
    v0a[:, 1] = lower
    v0b[:, 0] = upper

    def narrow(number, start, width, trials, part):
        step = width / (trials + 1)
        part[...] = jnp.zeros(part.shape, F32)
        for trial in range(trials):
            middle = start + (trial + 1) * step
            tried = jnp.minimum(jnp.maximum(v0a[:, 0] + middle[None], v0a[:, 1]), v0b[:, 0])
            part[trial : trial + 1] = jnp.sum(fold(tried), axis=0, keepdims=True)
        sums = jnp.sum(part[...], axis=1, keepdims=True)
        own = iota(part.shape, 0) == iota(part.shape, 1)
        row = jnp.sum(jnp.where(own, sums, 0.0), axis=0, keepdims=True)
        volumes = total_of(number, row)
        kept = (spot < trials) & jnp.logical_not(volumes > target)
        below = jnp.sum(kept.astype(F32), axis=1, keepdims=True)
        return start + below * step, step

    start, width = jnp.full((1, 1), -2.0, F32), 4.0
    start, width = narrow(1, start, width, FIRST, a_part)
    start, width = narrow(2, start, width, SECOND, b_part)
    multiplier = start + width * 0.5
    lower = jnp.maximum(0.0, old - move_limit)
    upper = jnp.minimum(1.0, old + move_limit)
    new_density[...] = jnp.where(
        design, jnp.minimum(jnp.maximum(field[...] + multiplier[None], lower), upper), old
    )


def plan_sums(counts):
    cx, cy, cz = counts
    if cx * cy * cz <= 64:
        return (cx * cy * cz,), True
    return (cy * cz, cx), False


def body(counts, density, kind):
    nx, ny, nz = density.shape
    cx, cy, cz = counts
    lines, _ = plan_sums(counts)
    sends = 3 * (sum(lines) - len(lines))
    wide = nx + 2 * RADIUS
    vm = lambda *shape: pltpu.VMEM(shape, F32)
    dma = lambda *shape: pltpu.SemaphoreType.DMA(shape)
    cube = (nx, ny, nz)
    half = (nx // 2, ny, nz)
    quarter = (nx // 4, ny, nz)
    pair = lambda planes: vm(planes, 2, ny, nz)

    scratch = [
        vm(*cube), vm(*cube), vm(*cube), vm(nx * ny, 3 * wide * ny), vm(nz + 128, nz),
        vm(3, wide, ny, nz + 128), vm(2, ny, 128), vm(2, 3, 3, ny, 128), dma(26), dma(26),
        pair(nx), pair(nx), pair(nx), vm(*cube), vm(*cube),
        pair(nx // 2), pair(nx // 2), pair(nx // 2), vm(*half), vm(*half),
        pair(nx // 4), pair(nx // 4), pair(nx // 4), vm(*quarter),
        vm(2, 2, ny, nz), vm(2, 2, ny, nz),
        vm(2, 2, 2 * nx, nz), vm(2, 2 * nx, nz), vm(2, 2 * nx, nz),
        vm(2, 2, 2, ny, 128), vm(2, 2, ny, 128), vm(2, 2, ny, 128), dma(2, 6), dma(2, 6),
        vm(FIRST + 1, 128), vm(SECOND + 1, 128), vm(3, 1, 128), vm(3, 1, 128),
        vm(3, lines[0], 1, 128), vm(3, lines[-1], 1, 128),
        dma(sends), dma(sends),
    ]
    spec = pl.BlockSpec(memory_space=pltpu.VMEM)
    return pl.pallas_call(
        functools.partial(kernel, counts),
        out_shape=[jax.ShapeDtypeStruct(cube, F32)] * 3,
        in_specs=[spec] * 2,
        out_specs=[spec] * 3,
        scratch_shapes=scratch,
        compiler_params=pltpu.CompilerParams(
            collective_id=0, has_side_effects=True, vmem_limit_bytes=40 * 1024 * 1024
        ),
    )(density, kind)


def solution(mesh):
    counts = tuple(mesh.shape[name] for name in ("gx", "gy", "gz"))

    def run(density, kind):
        return tuple(body(counts, density, kind))

    return jax.shard_map(
        run,
        mesh=mesh,
        in_specs=(P("gx", "gy", "gz"), P("gx", "gy", "gz")),
        out_specs=(P("gx", "gy", "gz"), P("gx", "gy", "gz"), P("gx", "gy", "gz")),
        check_vma=False,
    )
```

```python
import functools

import jax
import jax.numpy as jnp
from jax import lax
from jax.experimental import pallas as pl
from jax.experimental.pallas import tpu as pltpu
from jax.sharding import PartitionSpec as P

RADIUS = 6
LEVELS = 3
CYCLES = 2
COARSE_SWEEPS = 4
BISECT = 9

penalty_solid = 0.2
penalty_fluid = 0.001
convexity = 0.1
damping = 0.8
step_size = 0.1
move_limit = 0.2
volume_fraction = 0.45
epsilon = 1e-06

MESH = pl.DeviceIdType.MESH
F32 = jnp.float32
FIRST = 31
SECOND = 15


def iota(shape, dim):
    return lax.broadcasted_iota(jnp.int32, shape, dim)


def turn(values, shift, dim):
    shift = shift % values.shape[dim]
    return values if shift == 0 else pltpu.roll(values, shift, dim)


def restrict_pair(pair, stride):
    dy, dz = pair.ndim - 2, pair.ndim - 1
    low = ((iota(pair.shape, dy) // stride) & 1) == 0
    pair = pair + jnp.where(low, turn(pair, -stride, dy), turn(pair, stride, dy))
    low = ((iota(pair.shape, dz) // stride) & 1) == 0
    pair = pair + jnp.where(low, turn(pair, -stride, dz), turn(pair, stride, dz))
    return pair * 0.125


def edge_weight(position, total):
    low = jnp.maximum(RADIUS - position, 0)
    high = jnp.maximum(RADIUS - (total - 1 - position), 0)
    top = (RADIUS + 1) ** 2
    return (top - ((low * (low + 1)) >> 1) - ((high * (high + 1)) >> 1)).astype(F32)


def kernel(
    counts, density, kind, new_density, velocity, adjoint,
    field, filtered, normal, weight_y, weight_z,
    padded, fz_out, fz_in, f_send, f_recv,
    v0a, v0b, s0, diag0, damp0, v1a, v1b, s1, diag1, damp1, v2a, v2b, s2, damp2,
    c_out, cz_out, c_in, cz_in, c_force, c_damp, c_a, c_b, c_send, c_recv,
    mx_lo, mx_hi, my_out, my_lo, my_hi, mz_out, mz_lo, mz_hi, m_send, m_recv,
    a_part, b_part, r_out, r_mid, r_one, r_two, r_send, r_recv,
):
    nx, ny, nz = density.shape
    cx, cy, cz = counts
    ix, iy, iz = lax.axis_index("gx"), lax.axis_index("gy"), lax.axis_index("gz")
    lines, one_stage = plan_sums(counts)
    if one_stage:
        places = ((ix * cy + iy) * cz + iz,)
    else:
        places = (iy * cz + iz, ix)
    plane_size = cy * cz

    def device_of(flat):
        rest = lax.rem(flat, plane_size)
        return {"gx": flat // plane_size, "gy": rest // cz, "gz": lax.rem(rest, cz)}

    def peer_of(stage, step):
        if one_stage:
            return device_of(lax.rem(places[0] + step, lines[0]))
        if stage == 0:
            other = lax.rem(places[0] + step, lines[0])
            return {"gy": other // cz, "gz": lax.rem(other, cz)}
        return {"gx": lax.rem(ix + step, cx)}

    has_up = (ix < cx - 1, iy < cy - 1, iz < cz - 1)
    has_down = (ix > 0, iy > 0, iz > 0)
    names = ("gx", "gy", "gz")
    index = (ix, iy, iz)

    def clear(absent, refs):
        @pl.when(jnp.logical_not(absent))
        def _():
            for ref in refs:
                ref[...] = jnp.zeros(ref.shape, F32)

    clear(has_down[0], (mx_lo,))
    clear(has_up[0], (mx_hi,))
    clear(has_down[1], (my_lo,))
    clear(has_up[1], (my_hi,))
    clear(has_down[2], (mz_lo,))
    clear(has_up[2], (mz_hi,))
    padded[...] = jnp.zeros(padded.shape, F32)
    fz_in[...] = jnp.zeros(fz_in.shape, F32)
    c_in[...] = jnp.zeros(c_in.shape, F32)
    cz_in[...] = jnp.zeros(cz_in.shape, F32)

    barrier = pltpu.get_barrier_semaphore()
    devices = cx * cy * cz
    me = (ix * cy + iy) * cz + iz

    def greet(step):
        other = device_of(lax.rem(me + step, devices))
        pl.semaphore_signal(barrier, inc=1, device_id=other, device_id_type=MESH)

    if one_stage:
        for step in range(1, devices):
            greet(step)
    else:
        lax.fori_loop(1, devices, lambda step, none: (greet(step), none)[1], 0)

    field[...] = density[...]
    shape = (nx, ny, nz)
    normal[...] = 1.0 / (
        edge_weight(iota(shape, 0) + ix * nx, cx * nx)
        * edge_weight(iota(shape, 1) + iy * ny, cy * ny)
        * edge_weight(iota(shape, 2) + iz * nz, cz * nz)
    )
    rows = nx * ny
    wide = nx + 2 * RADIUS
    r, c = iota((rows, 3 * wide * ny), 0), iota((rows, 3 * wide * ny), 1)
    block = c // (wide * ny)
    inner = c - block * (wide * ny)
    gap_y = jnp.abs((block - 1) * ny + inner % ny - r % ny)
    gap_x = jnp.abs(inner // ny - RADIUS - r // ny)
    top = RADIUS + 1
    weight_y[...] = (jnp.maximum(top - gap_y, 0) * jnp.maximum(top - gap_x, 0)).astype(F32)
    r, c = iota((nz + 128, nz), 0), iota((nz + 128, nz), 1)
    at = jnp.where(r < 8, nz + r, jnp.where(r < 120, -1000, r - 128))
    weight_z[...] = jnp.maximum(RADIUS + 1 - jnp.abs(at - c), 0).astype(F32)
    for plane in range(nx):
        s0[plane] = jnp.stack(
            [(kind[plane] == 14).astype(F32), (kind[plane] == 15).astype(F32)]
        )

    pl.semaphore_wait(barrier, devices - 1)

    def swap(sends, send_sems, recv_sems):
        copies = []
        for axis, up_src, up_dst, down_src, down_dst in sends:
            for way, src, dst in ((0, up_src, up_dst), (1, down_src, down_dst)):
                def make(axis=axis, way=way, src=src, dst=dst):
                    to = index[axis] + 1 - 2 * way
                    return pltpu.make_async_remote_copy(
                        src_ref=src,
                        dst_ref=dst,
                        send_sem=send_sems.at[2 * axis + way],
                        recv_sem=recv_sems.at[2 * axis + way],
                        device_id={names[axis]: to},
                        device_id_type=MESH,
                    )
                sent = (has_up, has_down)[way][axis]
                got = (has_down, has_up)[way][axis]
                copies.append((make, sent, got))

        for make, sent, got in copies:
            @pl.when(sent)
            def _(make=make):
                make().start()

        for make, sent, got in copies:
            @pl.when(got)
            def _(make=make):
                make().wait_recv()

        for make, sent, got in copies:
            @pl.when(sent)
            def _(make=make):
                make().wait_send()

    def pack_z(source, planes, out):
        tail = head = None
        for plane in range(planes):
            full = source[plane]
            dim = full.ndim - 1
            last = turn(full[..., nz - 128 :], 8 * plane + 8, dim)
            first = turn(full[..., :128], 8 * plane, dim)
            mine = (iota(last.shape, dim) >> 3) == plane
            tail = last if tail is None else jnp.where(mine, last, tail)
            head = first if head is None else jnp.where(mine, first, head)
        out[0] = tail
        out[1] = head

    ways = [
        (dx, dy, dz)
        for dz in (0, 1, -1) for dx in (0, 1, -1) for dy in (1, -1, 0) if (dx, dy, dz) != (0, 0, 0)
    ]

    def reachable(way, sign):
        there = None
        for axis in range(3):
            if way[axis]:
                side = (has_up if way[axis] * sign > 0 else has_down)[axis]
                there = side if there is None else jnp.logical_and(there, side)
        return there

    def spread():
        padded[1, RADIUS : RADIUS + nx, :, 128:] = field[...]
        pack_z(field, nx, fz_out)

        def make(number, way):
            dx, dy, dz = way
            if dz == 0:
                start = nx - RADIUS if dx > 0 else 0
                at = 0 if dx > 0 else RADIUS + nx if dx < 0 else RADIUS
                size = RADIUS if dx else nx
                src = field.at[pl.ds(start, size)]
                dst = padded.at[1 - dy, pl.ds(at, size), :, pl.ds(128, nz)]
            else:
                which = 0 if dz > 0 else 1
                src = fz_out.at[which]
                dst = fz_in.at[which, 1 - dy, 1 - dx]
            there = {names[axis]: index[axis] + way[axis] for axis in range(3) if way[axis]}
            return pltpu.make_async_remote_copy(
                src_ref=src, dst_ref=dst, send_sem=f_send.at[number],
                recv_sem=f_recv.at[number], device_id=there, device_id_type=MESH,
            )

        for number, way in enumerate(ways):
            @pl.when(reachable(way, 1))
            def _(number=number, way=way):
                make(number, way).start()

        for number, way in reversed(list(enumerate(ways))):
            @pl.when(reachable(way, -1))
            def _(number=number, way=way):
                make(number, way).wait_recv()

        for number, way in enumerate(ways):
            @pl.when(reachable(way, 1))
            def _(number=number, way=way):
                make(number, way).wait_send()

        lane = iota((ny, 128), 1)
        for dy in range(3):
            for plane in range(wide):
                if plane < RADIUS:
                    dx, origin = 0, nx - RADIUS + plane
                elif plane < RADIUS + nx:
                    dx, origin = 1, plane - RADIUS
                else:
                    dx, origin = 2, plane - RADIUS - nx
                low = turn(fz_in[0, dy, dx], 120 - 8 * origin, 1)
                high = turn(fz_in[1, dy, dx], -8 * origin, 1)
                padded[dy, plane, :, 0:128] = jnp.where(
                    lane >= 120, low, jnp.where(lane < 8, high, 0.0)
                )
        mixed = jnp.dot(
            weight_y[...], padded[...].reshape(3 * wide * ny, nz + 128),
            precision=lax.Precision.HIGHEST, preferred_element_type=F32,
        )
        field[...] = jnp.dot(
            mixed, weight_z[...], precision=lax.Precision.HIGHEST, preferred_element_type=F32
        ).reshape(nx, ny, nz)

    spread()
    smooth = field[...] * normal[...]
    filtered[...] = smooth
    interp = penalty_solid + (penalty_fluid - penalty_solid) * smooth * (1.0 + convexity) / (
        smooth + convexity
    )
    kinds = kind[...]
    penalty = jnp.where(
        kinds < 13, interp, jnp.where(kinds == 13, penalty_solid, penalty_fluid)
    )
    diag0[...] = 6.0 + penalty
    damp0[...] = damping / (6.0 + penalty)
    level1 = []
    for plane in range(nx // 2):
        coarse = restrict_pair(penalty[2 * plane] + penalty[2 * plane + 1], 1)
        level1.append(coarse)
        diag1[plane] = 1.5 + coarse
        damp1[plane] = damping / (1.5 + coarse)
    for plane in range(nx // 4):
        coarse = restrict_pair(level1[2 * plane] + level1[2 * plane + 1], 2)
        damp2[plane] = damping / (0.375 + coarse)

    few = nx // 4
    deep = cy == 2 and 3 <= few <= 8 and ny == 8
    reach = COARSE_SWEEPS - 1
    near = [
        (dx, dy, dz)
        for dz in (0, 1, -1) for dx in (0, 1, -1) for dy in (1, 0) if (dx, dy, dz) != (0, 0, 0)
    ]

    def gather_copy(turn_number, number, way):
        dx, dy, dz = way
        if dz == 0:
            size = reach if dx else few
            start = few - reach if dx > 0 else 0
            at = 0 if dx > 0 else reach + few if dx < 0 else reach
            src = c_out.at[turn_number, pl.ds(start, size)]
            dst = c_in.at[turn_number, dy, pl.ds(at, size)]
        else:
            which = 0 if dz > 0 else 1
            src = cz_out.at[turn_number, which]
            dst = cz_in.at[turn_number, which, dy, 1 - dx]
        there = {}
        if dx:
            there["gx"] = ix + dx
        if dy:
            there["gy"] = 1 - iy
        if dz:
            there["gz"] = iz + dz
        return pltpu.make_async_remote_copy(
            src_ref=src, dst_ref=dst, send_sem=c_send.at[turn_number, number],
            recv_sem=c_recv.at[turn_number, number], device_id=there, device_id_type=MESH,
        )

    def guarded(way, sign, act):
        side = reachable((way[0], 0, way[2]), sign)
        if side is None:
            act()
        else:
            pl.when(side)(act)

    def gather_start(turn_number, first, second):
        row = iota((ny, nz), 0)
        other = ((row & 1) ^ (row >> 2)) == 1
        spot = iota((ny, 128), 1)
        tail = head = None
        for plane in range(few):
            a, b = first(plane), second(plane)
            a = jnp.where(other, turn(a, 4, 0), a)
            b = jnp.where(other, turn(b, 4, 0), b)
            tile = jnp.where(row < 4, a, b)
            c_out[turn_number, plane] = tile
            last = turn(tile[:, nz - 128 :], 16 * plane + 16, 1)
            begin = turn(tile[:, :128], 16 * plane, 1)
            mine = (spot >> 4) == plane
            tail = last if tail is None else jnp.where(mine, last, tail)
            head = begin if head is None else jnp.where(mine, begin, head)
        cz_out[turn_number, 0] = tail
        cz_out[turn_number, 1] = head
        for number, way in enumerate(near):
            guarded(way, 1, lambda n=number, w=way: gather_copy(turn_number, n, w).start())

    def gather_finish(turn_number, target):
        for number, way in enumerate(near):
            guarded(way, -1, lambda n=number, w=way: gather_copy(turn_number, n, w).wait_recv())
        for number, way in enumerate(near):
            guarded(way, 1, lambda n=number, w=way: gather_copy(turn_number, n, w).wait_send())
        spot = iota((ny, 128), 1)
        mine = ((iota((ny, nz), 0) >> 1) & 1) == iy
        here = ((iota((ny, 128), 0) >> 1) & 1) == iy
        for plane in range(few + 2 * reach):
            if plane < reach:
                dx, origin = 0, few - reach + plane
            elif plane < reach + few:
                dx, origin = 1, plane - reach
            else:
                dx, origin = 2, plane - reach - few
            own = c_out[turn_number, origin] if dx == 1 else c_in[turn_number, 0, plane]
            low = jnp.where(here, cz_in[turn_number, 0, 0, dx], cz_in[turn_number, 0, 1, dx])
            high = jnp.where(here, cz_in[turn_number, 1, 0, dx], cz_in[turn_number, 1, 1, dx])
            low = turn(low, 112 - 16 * origin, 1)
            high = turn(high, -16 * origin, 1)
            target[plane, :, 0:128] = jnp.where(
                spot >= 116, low, jnp.where(spot < 12, high, 0.0)
            )
            target[plane, :, 128:] = jnp.where(mine, own, c_in[turn_number, 1, plane])

    def coarse_solve(turn_number):
        gather_start(turn_number, lambda plane: s2[plane, 0], lambda plane: s2[plane, 1])
        if turn_number == 1:
            gather_finish(0, c_damp)
        gather_finish(turn_number, c_force)
        tall = few + 2 * reach
        for plane in range(tall):
            c_a[plane] = c_damp[plane] * c_force[plane]
        row = iota((ny, nz + 128), 0) & 3
        src, dst = c_a, c_b
        for sweep in range(1, reach + 1):
            for plane in range(sweep, tall - sweep):
                centre = src[plane]
                total = src[plane - 1] + src[plane + 1]
                total = total + jnp.where(row >= 1, turn(centre, 1, 0), 0.0)
                total = total + jnp.where(row <= 2, turn(centre, -1, 0), 0.0)
                total = total + turn(centre, 4, 1) + turn(centre, -4, 1)
                dst[plane] = (1.0 - damping) * centre + c_damp[plane] * (
                    c_force[plane] + 0.0625 * total
                )
            src, dst = dst, src
        row = iota((ny, nz), 0)
        upper_half = (row * 0 + iy) == 1
        for plane in range(few):
            tile = src[reach + plane, :, 128:]
            tile = jnp.where(upper_half, turn(tile, -2, 0), tile)
            v2a[plane] = jnp.stack([
                jnp.where(
                    row < 4,
                    jnp.broadcast_to(tile[4 * which : 4 * which + 1], (ny, nz)),
                    jnp.broadcast_to(tile[4 * which + 1 : 4 * which + 2], (ny, nz)),
                )
                for which in range(2)
            ])

    if deep:
        gather_start(0, lambda plane: damp2[plane], lambda plane: damp2[plane])

    sub = iota((2, ny, nz), 1)
    lane = iota((2, ny, 128), 2)
    rounds = [0]

    def exchange(source, planes):
        parity = rounds[0] % 2
        rounds[0] += 1
        for plane in range(planes):
            for which in range(2):
                row = 2 * plane + which
                my_out[parity, 0, row : row + 1] = source[plane, which, ny - 1 : ny]
                my_out[parity, 1, row : row + 1] = source[plane, which, 0:1]
        pack_z(source, planes, mz_out.at[parity])
        part = pl.ds(0, 2 * planes)
        swap(
            [
                (0, source.at[planes - 1], mx_lo.at[parity], source.at[0], mx_hi.at[parity]),
                (1, my_out.at[parity, 0, part], my_lo.at[parity, part],
                 my_out.at[parity, 1, part], my_hi.at[parity, part]),
                (2, mz_out.at[parity, 0], mz_lo.at[parity],
                 mz_out.at[parity, 1], mz_hi.at[parity]),
            ],
            m_send.at[parity], m_recv.at[parity],
        )
        return parity

    def both(ref, parity, plane):
        return jnp.stack(
            [
                jnp.broadcast_to(ref[parity, 2 * plane + which : 2 * plane + which + 1], (ny, nz))
                for which in range(2)
            ]
        )

    def beside(source, planes, stride, parity, plane):
        centre = source[plane]
        low = source[plane - 1] if plane else mx_lo[parity]
        high = source[plane + 1] if plane < planes - 1 else mx_hi[parity]
        total = low + high
        low = jnp.where(sub < stride, both(my_lo, parity, plane), turn(centre, stride, 1))
        high = jnp.where(sub >= ny - stride, both(my_hi, parity, plane), turn(centre, -stride, 1))
        total = total + low + high
        low = turn(centre, stride, 2)
        edge = turn(mz_lo[parity], stride - 8 - 8 * plane, 2)
        low = jnp.concatenate(
            [jnp.where(lane < stride, edge, low[..., :128]), low[..., 128:]], axis=2
        )
        high = turn(centre, -stride, 2)
        edge = turn(mz_hi[parity], 128 - stride - 8 * plane, 2)
        high = jnp.concatenate(
            [high[..., : nz - 128], jnp.where(lane >= 128 - stride, edge, high[..., nz - 128 :])],
            axis=2,
        )
        return total + low + high

    def relax(source, target, forcing, damp, planes, stride, scale):
        parity = exchange(source, planes)
        for plane in range(planes):
            total = beside(source, planes, stride, parity, plane)
            target[plane] = (1.0 - damping) * source[plane] + damp[plane][None] * (
                forcing[plane] + scale * total
            )

    def misfit(source, coarse, forcing, diag, planes, stride, scale):
        parity = exchange(source, planes)
        for pair in range(planes // 2):
            total = None
            for plane in (2 * pair, 2 * pair + 1):
                rest = (
                    forcing[plane]
                    - diag[plane][None] * source[plane]
                    + scale * beside(source, planes, stride, parity, plane)
                )
                total = rest if total is None else total + rest
            coarse[pair] = restrict_pair(total, stride)

    now, later = v0a, v0b
    for cycle in range(CYCLES):
        if cycle == 0:
            for plane in range(nx):
                now[plane] = damp0[plane][None] * s0[plane]
        else:
            relax(now, later, s0, damp0, nx, 1, 1.0)
            now, later = later, now
        misfit(now, s1, s0, diag0, nx, 1, 1.0)
        for plane in range(nx // 2):
            v1a[plane] = damp1[plane][None] * s1[plane]
        misfit(v1a, s2, s1, diag1, nx // 2, 2, 0.25)
        here, there = v2a, v2b
        if deep:
            coarse_solve(cycle + 1)
        else:
            for plane in range(nx // 4):
                v2a[plane] = damp2[plane][None] * s2[plane]
            for sweep in range(COARSE_SWEEPS - 1):
                relax(here, there, s2, damp2, nx // 4, 4, 0.0625)
                here, there = there, here
        for plane in range(nx // 2):
            v1a[plane] = v1a[plane] + here[plane // 2]
        relax(v1a, v1b, s1, damp1, nx // 2, 2, 0.25)
        for plane in range(nx):
            now[plane] = now[plane] + v1b[plane // 2]
        relax(now, later, s0, damp0, nx, 1, 1.0)
        now, later = later, now

    for plane in range(nx):
        flow, dual = now[plane, 0], now[plane, 1]
        velocity[plane] = flow
        adjoint[plane] = dual
        bent = filtered[plane] + convexity
        slope = (penalty_fluid - penalty_solid) * (1.0 + convexity) * convexity / (bent * bent)
        field[plane] = jnp.where(kind[plane] < 13, dual * flow * slope, 0.0) * normal[plane]
    spread()

    sems = [0]

    def total_of(number, row):
        for stage, size in enumerate(lines):
            source = (r_out, r_mid)[stage].at[number]
            target = (r_one, r_two)[stage].at[number]
            source[...] = row
            copies = []
            for step in range(1, size):
                copy = pltpu.make_async_remote_copy(
                    src_ref=source,
                    dst_ref=target.at[places[stage]],
                    send_sem=r_send.at[sems[0]],
                    recv_sem=r_recv.at[sems[0]],
                    device_id=peer_of(stage, step),
                    device_id_type=MESH,
                )
                sems[0] += 1
                copy.start()
                copies.append(copy)
            target[places[stage]] = row
            for copy in copies:
                copy.wait_recv()
            row = target[0]
            for other in range(1, size):
                row = row + target[other]
            for copy in copies:
                copy.wait_send()
        return row

    def fold(values):
        values = jnp.sum(values, axis=0)
        total = values[:, :128]
        for start in range(128, nz, 128):
            total = total + values[:, start : start + 128]
        return total

    def whole(values):
        return jnp.sum(jnp.sum(values, axis=0, keepdims=True), axis=1, keepdims=True)

    design = kind[...] < 13
    sensitivity = field[...]
    spot = iota((1, 128), 1)
    squares = whole(fold(sensitivity * sensitivity))
    designs = whole(fold(design.astype(F32)))
    stats = total_of(0, jnp.where(spot == 0, squares, jnp.where(spot == 1, designs, 0.0)))
    cells = float(cx * nx * cy * ny * cz * nz)
    spreading = jnp.sqrt(whole(jnp.where(spot == 0, stats, 0.0)) / cells + epsilon)
    target = volume_fraction * whole(jnp.where(spot == 1, stats, 0.0))
    old = density[...]
    field[...] = old - step_size * (field[...] / spreading[None])
    base = jnp.where(design, field[...], 0.0)
    lower = jnp.where(design, jnp.maximum(0.0, old - move_limit), 0.0)
    upper = jnp.where(design, jnp.minimum(1.0, old + move_limit), 0.0)
    v0a[:, 0] = base
    v0a[:, 1] = lower
    v0b[:, 0] = upper

    def narrow(number, start, width, trials, part):
        step = width / (trials + 1)
        part[...] = jnp.zeros(part.shape, F32)
        for trial in range(trials):
            middle = start + (trial + 1) * step
            tried = jnp.minimum(jnp.maximum(v0a[:, 0] + middle[None], v0a[:, 1]), v0b[:, 0])
            part[trial : trial + 1] = jnp.sum(fold(tried), axis=0, keepdims=True)
        sums = jnp.sum(part[...], axis=1, keepdims=True)
        own = iota(part.shape, 0) == iota(part.shape, 1)
        row = jnp.sum(jnp.where(own, sums, 0.0), axis=0, keepdims=True)
        volumes = total_of(number, row)
        kept = (spot < trials) & jnp.logical_not(volumes > target)
        below = jnp.sum(kept.astype(F32), axis=1, keepdims=True)
        return start + below * step, step

    start, width = jnp.full((1, 1), -2.0, F32), 4.0
    start, width = narrow(1, start, width, FIRST, a_part)
    start, width = narrow(2, start, width, SECOND, b_part)
    multiplier = start + width * 0.5
    lower = jnp.maximum(0.0, old - move_limit)
    upper = jnp.minimum(1.0, old + move_limit)
    new_density[...] = jnp.where(
        design, jnp.minimum(jnp.maximum(field[...] + multiplier[None], lower), upper), old
    )


def plan_sums(counts):
    cx, cy, cz = counts
    if cx * cy * cz <= 64:
        return (cx * cy * cz,), True
    return (cy * cz, cx), False


def body(counts, density, kind):
    nx, ny, nz = density.shape
    cx, cy, cz = counts
    lines, _ = plan_sums(counts)
    sends = 3 * (sum(lines) - len(lines))
    wide = nx + 2 * RADIUS
    few = nx // 4
    tall = few + 2 * (COARSE_SWEEPS - 1)
    vm = lambda *shape: pltpu.VMEM(shape, F32)
    dma = lambda *shape: pltpu.SemaphoreType.DMA(shape)
    cube = (nx, ny, nz)
    half = (nx // 2, ny, nz)
    quarter = (nx // 4, ny, nz)
    pair = lambda planes: vm(planes, 2, ny, nz)

    scratch = [
        vm(*cube), vm(*cube), vm(*cube), vm(nx * ny, 3 * wide * ny), vm(nz + 128, nz),
        vm(3, wide, ny, nz + 128), vm(2, ny, 128), vm(2, 3, 3, ny, 128), dma(26), dma(26),
        pair(nx), pair(nx), pair(nx), vm(*cube), vm(*cube),
        pair(nx // 2), pair(nx // 2), pair(nx // 2), vm(*half), vm(*half),
        pair(nx // 4), pair(nx // 4), pair(nx // 4), vm(*quarter),
        vm(3, few, ny, nz), vm(3, 2, ny, 128), vm(3, 2, tall, ny, nz), vm(3, 2, 2, 3, ny, 128),
        vm(tall, ny, nz + 128), vm(tall, ny, nz + 128), vm(tall, ny, nz + 128),
        vm(tall, ny, nz + 128), dma(3, 17), dma(3, 17),
        vm(2, 2, ny, nz), vm(2, 2, ny, nz),
        vm(2, 2, 2 * nx, nz), vm(2, 2 * nx, nz), vm(2, 2 * nx, nz),
        vm(2, 2, 2, ny, 128), vm(2, 2, ny, 128), vm(2, 2, ny, 128), dma(2, 6), dma(2, 6),
        vm(FIRST + 1, 128), vm(SECOND + 1, 128), vm(3, 1, 128), vm(3, 1, 128),
        vm(3, lines[0], 1, 128), vm(3, lines[-1], 1, 128),
        dma(sends), dma(sends),
    ]
    spec = pl.BlockSpec(memory_space=pltpu.VMEM)
    return pl.pallas_call(
        functools.partial(kernel, counts),
        out_shape=[jax.ShapeDtypeStruct(cube, F32)] * 3,
        in_specs=[spec] * 2,
        out_specs=[spec] * 3,
        scratch_shapes=scratch,
        compiler_params=pltpu.CompilerParams(
            collective_id=0, has_side_effects=True, vmem_limit_bytes=40 * 1024 * 1024
        ),
    )(density, kind)


def solution(mesh):
    counts = tuple(mesh.shape[name] for name in ("gx", "gy", "gz"))

    def run(density, kind):
        return tuple(body(counts, density, kind))

    return jax.shard_map(
        run,
        mesh=mesh,
        in_specs=(P("gx", "gy", "gz"), P("gx", "gy", "gz")),
        out_specs=(P("gx", "gy", "gz"), P("gx", "gy", "gz"), P("gx", "gy", "gz")),
        check_vma=False,
    )
```
